256 devices in a mesh: feat: 16 (over x_hi, z), ex: 16 (over y, x_lo, core).
Axes of the slice: x: 4 (x_hi: 2, x_lo: 2; x = x_hi * 2 + x_lo), y: 4, z: 8, core: 2. Of those that a mesh axis runs over, the one named last changes fastest.
Arguments:
- queries: bfloat16 [2048, 32768], P('ex', 'feat'), may hold values from -6 to 6
- train_grads: bfloat16 [16384, 32768], P('ex', 'feat'), may hold values from -0.03125 to 0.03125
Outputs:
- scores: float32 [2048, 16384], P('feat', 'ex')
The draws below stay inside these ranges and needn't reach their ends.
All inputs are finite; a program needn't handle non-finite values.
Results may differ from the reference program's by a relative error of at most 0.0003.
Values may be sent and summed in bfloat16 or wider, within the bound.
No kernel may reach another device: no remote copies, remote signals or barrier semaphores. Data moves between devices by JAX's collectives and lax.ppermute only.
A program may use at most 64 MiB of HBM per device.

```python
import jax
import jax.numpy as jnp
from jax import lax

QB = 128
TR_DEV = 1024
FEATS = 32768
QUERIES = 2048
TRAIN = 16384
N_EX = 16


def spiked(entries, rng, source, target, blocks, factor):
    owner, partner = [(jnp.arange(entries.shape[axis_at]) // (entries.shape[axis_at] // blocks)).reshape([-1 if axis == axis_at else 1 for axis in range(entries.ndim)]) for axis_at in (source, target)]
    chosen = jax.random.permutation(rng, blocks)[partner]
    strong = (owner == chosen) | (owner == (partner + blocks // 2) % blocks)
    return jnp.where(strong, factor * entries, entries)


def block_levels(stream_key, extent, split, low, top_value):
    loudness, own = 1.0, jax.random.fold_in(stream_key, 6)
    for dim, blocks in split:
        draws = jnp.exp(jax.random.uniform(jax.random.fold_in(own, dim), (blocks,), jnp.float32, low / len(split), top_value / len(split)))
        loudness = loudness * jnp.repeat(draws, extent[dim] // blocks).reshape([-1 if axis == dim else 1 for axis in range(len(extent))])
    return loudness


def centred(rng, dims, deviation, bound, split=(), dtype=jnp.bfloat16):
    entries = deviation * jax.random.normal(rng, dims, jnp.float32)
    if split:
        entries = entries * block_levels(rng, dims, split, -0.22, 0.18)
    return jnp.clip(entries, -bound, bound).astype(dtype)


def noise_with(stream_key, dims, spread, limit, pieces, heavy, dtype=jnp.bfloat16):
    result = spread * jax.random.normal(stream_key, dims, jnp.float32)
    if pieces:
        result = result * block_levels(stream_key, dims, pieces, -0.22, 0.18)
    return jnp.clip(spiked(result, jax.random.fold_in(stream_key, 3), *heavy), -limit, limit).astype(dtype)


def setup_inputs(seed: int = 0) -> dict:
    key_of = jax.random.split(jax.random.key(seed), 3)
    return {
        "queries": noise_with(key_of[0], (QUERIES, FEATS), 1.0, 6.0, ((0, 16), (1, 16)), (1, 0, 16, 2.0)),
        "train_grads": centred(key_of[1], (TRAIN, FEATS), FEATS ** -0.5, 0.03125, ((0, 16), (1, 16))),
    }


def reference(queries, train_grads):
    query_full = queries.astype(jnp.float32)
    blocks = train_grads.reshape(N_EX, TR_DEV, FEATS)

    def score_block(block):
        return jnp.dot(query_full, block.astype(jnp.float32).T)

    parts = lax.map(score_block, blocks)
    return jnp.transpose(parts, (1, 0, 2)).reshape(QB * N_EX, TR_DEV * N_EX)
```

```python
import jax
import jax.numpy as jnp
from jax import lax
from jax.sharding import Mesh
from jax.sharding import PartitionSpec as P

EX = ("y", "xl", "c")
FEAT = ("xh", "z")


def on_device(queries, train_grads):
    everyone = lax.all_gather(queries, EX, tiled=True)
    part = lax.dot_general(
        everyone, train_grads, (((1,), (1,)), ((), ())), preferred_element_type=jnp.float32
    )
    rows = queries.shape[0]
    part = part.reshape(2, 8 * rows, train_grads.shape[0])
    part = lax.psum_scatter(part, "z", scatter_dimension=1, tiled=True)
    return lax.psum_scatter(part, "xh", scatter_dimension=0, tiled=False)


def solution(mesh):
    fine = Mesh(mesh.devices.reshape(2, 8, 4, 2, 2), FEAT + EX)
    return jax.shard_map(
        on_device,
        mesh=fine,
        in_specs=(P(EX, FEAT), P(EX, FEAT)),
        out_specs=P(FEAT, EX),
        check_vma=False,
    )
```

```python
import jax
import jax.numpy as jnp
from jax import lax
from jax.sharding import Mesh
from jax.sharding import PartitionSpec as P

EX = ("y", "xl", "c")
FEAT = ("xh", "z")
CHUNKS = 4


def swap(block, axis, bits):
    return lax.ppermute(block, axis, [(i, i ^ bits) for i in range(lax.axis_size(axis))])


def turn(block, step):
    size = lax.axis_size("z")
    return lax.ppermute(block, "z", [(i, (i + step) % size) for i in range(size)])


def gathered(rows):
    pair = jnp.stack([rows, swap(rows, "xl", 1)])
    near = swap(pair, "y", 1)
    back = swap(pair, "y", 3)
    far = [swap(near[:1], "y", 3), swap(back[1:], "y", 1)]
    mine = jnp.concatenate([pair, near, *far, back])
    return jnp.stack([mine, swap(mine, "c", 1)])


def reduced(part, forward):
    half = part.shape[-1] // 2
    ex = lax.axis_index("y") * 4 + lax.axis_index("xl") * 2 + lax.axis_index("c")
    z = lax.axis_index("z")
    mine = (ex // 8) ^ lax.axis_index("xh")
    left, right = part[..., :half], part[..., half:]

    def side(array, axis, which):
        return lax.dynamic_index_in_dim(array, which, axis, keepdims=False)

    left = side(left, 1, mine) + swap(side(left, 1, 1 - mine), "xh", 1)

    def term(distance):
        slot = ((z + distance) % 8) ^ (ex % 8)
        low = side(side(left, 0, slot % 2), 0, slot // 2)
        high = side(side(right, 0, slot % 2), 1, slot // 2)
        return jnp.concatenate([low[None], high])

    def ring(step, hops):
        total = turn(term(step * hops), step)
        for hop in range(hops - 1, 0, -1):
            total = turn(total + term(step * hop), step)
        return total

    total = term(0) + ring(1, 4 if forward else 3) + ring(-1, 3 if forward else 4)
    low, high = total[0], total[1:]
    high = side(high, 0, mine) + swap(side(high, 0, 1 - mine), "xh", 1)
    return jnp.concatenate([low, high], axis=-1)


def on_device(queries, train_grads):
    count = queries.shape[0] // CHUNKS
    outs = []
    for chunk in range(CHUNKS):
        rows = gathered(queries[chunk * count : (chunk + 1) * count])
        part = lax.dot_general(
            rows.reshape(16 * count, -1), train_grads, (((1,), (1,)), ((), ())), preferred_element_type=jnp.float32
        )
        outs.append(reduced(part.reshape(2, 2, 4, count, -1), chunk % 2 == 0))
    return jnp.concatenate(outs)


def solution(mesh):
    fine = Mesh(mesh.devices.reshape(2, 8, 4, 2, 2), FEAT + EX)
    return jax.shard_map(
        on_device,
        mesh=fine,
        in_specs=(P(EX, FEAT), P(EX, FEAT)),
        out_specs=P(FEAT, EX),
        check_vma=False,
    )
```

```python
import jax
import jax.numpy as jnp
from jax import lax
from jax.sharding import Mesh
from jax.sharding import PartitionSpec as P

EX = ("y", "xl", "c")
FEAT = ("xh", "z")
PARTS = 2
LATE = 2
SYNC = True


def swap(block, axis, bits=1):
    return lax.ppermute(block, axis, [(i, i ^ bits) for i in range(lax.axis_size(axis))])


def turn(block, step):
    return lax.ppermute(block, "z", [(i, (i + step) % 8) for i in range(8)])


def pack(total):
    high = lax.reduce_precision(total, 8, 7)
    rest = jnp.round((total - high) / jnp.where(high == 0, 1.0, high) * 2048.0)
    half = total.shape[0] // 2
    both = rest[:half] * 17.0 + rest[half:]
    return jnp.concatenate([high, both]).astype(jnp.bfloat16)


def unpack(block):
    half = block.shape[0] // 3
    block = block.astype(jnp.float32)
    high, both = block[: 2 * half], block[2 * half :]
    first = jnp.round(both * (1 / 17.0))
    rest = jnp.concatenate([first, both - 17.0 * first])
    return high + high * rest * (1 / 2048.0)


def after(array, *others):
    return lax.optimization_barrier((array, *others))[0]


def tied(*arrays):
    return lax.optimization_barrier(arrays)


def gathered(queries, train_grads):
    rows, columns = queries.shape[0], train_grads.shape[0]
    half = rows // 2
    same, other = (jnp.zeros((8, rows, columns), jnp.float32) for _ in range(2))

    def add(part, slot, block):
        both = jnp.concatenate([block, swap(block, "c")])
        new = lax.dot_general(both, train_grads, (((1,), (1,)), ((), ())), preferred_element_type=jnp.float32)
        return lax.dynamic_update_slice(part, new.reshape(2, rows, columns), (slot, 0, 0))

    beside, near, back = swap(queries, "xl"), swap(queries, "y", 1), swap(queries, "y", 3)
    same = add(same, 0, queries)
    beside, near, back = tied(beside, near, back)
    near_beside, back_beside = swap(beside, "y", 1), swap(beside, "y", 3)
    same = add(same, 2, beside)
    same = add(same, 4, near)
    other = add(other, 4, back)
    near_beside, back_beside = tied(near_beside, back_beside)
    left = swap(jnp.concatenate([near[:half], near_beside[:half]]), "y", 3)
    right = swap(jnp.concatenate([back[half:], back_beside[half:]]), "y", 1)
    same = add(same, 6, near_beside)
    other = add(other, 6, back_beside)
    yield same
    (held,) = yield
    left, right = tied(left, right, held)[:2]
    other = add(other, 0, jnp.concatenate([left[:half], right[:half]]))
    other = add(other, 2, jnp.concatenate([left[half:], right[half:]]))
    yield other


class Ring:
    def __init__(self, part, long):
        self.ex = lax.axis_index("y") * 4 + lax.axis_index("xl") * 2 + lax.axis_index("c")
        self.z = lax.axis_index("z")
        self.part, self.long = part, long
        self.ahead = self.behind = None

    def term(self, distance):
        return lax.dynamic_index_in_dim(self.part, (self.z + distance) % 8 ^ self.ex % 8, 0, keepdims=False)

    def step(self, step):
        if step == 0:
            first = pack(self.term(4 * self.long))
            self.ahead = turn(first, self.long)
            return first
        hop = 4 - step
        ahead = unpack(self.ahead) + self.term(hop * self.long)
        behind = self.term(-hop * self.long)
        if step > 1:
            behind = unpack(self.behind) + behind
        if step == 3:
            return (ahead, behind) if self.long > 0 else (behind, ahead)
        ahead, behind = pack(ahead), pack(behind)
        return ahead, behind

    def send(self, ahead, behind):
        self.ahead, self.behind = turn(ahead, self.long), turn(behind, -self.long)


def on_device(queries, train_grads):
    flow = gathered(queries, train_grads)
    size = queries.shape[0] // PARTS

    def chains(i, part):
        return [Ring(part[:, k * size : k * size + size], 1 - 2 * i) for k in range(PARTS)]

    early = chains(0, next(flow))
    held = [ring.step(0) for ring in early]
    next(flow)
    late = chains(1, flow.send([held[0]]))
    firsts = [ring.step(0) for ring in late]
    if LATE:
        for ring, first in zip(early, firsts):
            ring.ahead = after(ring.ahead, firsts[0] if LATE == 1 else first)
    mine = lax.axis_index("xh") == lax.axis_index("y") // 2
    outs = [None] * PARTS
    for step in (1, 2):
        if step == 1:
            for k in range(PARTS):
                left, right = early[k].term(0), late[k].term(0)
                outs[k] = jnp.where(mine, left, right) + swap(jnp.where(mine, right, left), "xh")
        for k in range(PARTS):
            one, two = early[k].step(step), late[k].step(step)
            if SYNC:
                one, two = tied(one, two)
            else:
                one, two = tied(*one), tied(*two)
            early[k].send(*one)
            late[k].send(*two)
    for k in range(PARTS):
        one, two = early[k], late[k]
        one.ahead, outs[k] = tied(one.ahead, outs[k])
        sums = list(zip(one.step(3), two.step(3)))
        gives = tied(*(pack(jnp.where(mine, b, a)) for a, b in sums))
        keeps = [jnp.where(mine, a, b) + unpack(swap(give, "xh")) for (a, b), give in zip(sums, gives)]
        keeps = tied(*keeps)
        outs[k] += turn(keeps[0], 1) + turn(keeps[1], -1)
    return jnp.concatenate(outs)


def solution(mesh):
    fine = Mesh(mesh.devices.reshape(2, 8, 4, 2, 2), FEAT + EX)
    return jax.shard_map(
        on_device,
        mesh=fine,
        in_specs=(P(EX, FEAT), P(EX, FEAT)),
        out_specs=P(FEAT, EX),
        check_vma=False,
    )
```

```python
import jax
import jax.numpy as jnp
from jax import lax
from jax.sharding import Mesh
from jax.sharding import PartitionSpec as P

EX = ("y", "xl", "c")
FEAT = ("xh", "z")
PARTS = 2
LATE = 2
SYNC = True


def swap(block, axis, bits=1):
    return lax.ppermute(block, axis, [(i, i ^ bits) for i in range(lax.axis_size(axis))])


def turn(block, step):
    return lax.ppermute(block, "z", [(i, (i + step) % 8) for i in range(8)])


def pack(total):
    high = lax.reduce_precision(total, 8, 7)
    rest = jnp.round((total - high) / jnp.where(high == 0, 1.0, high) * 2048.0)
    half = total.shape[0] // 2
    both = rest[:half] * 17.0 + rest[half:]
    return jnp.concatenate([high, both]).astype(jnp.bfloat16)


def unpack(block):
    half = block.shape[0] // 3
    block = block.astype(jnp.float32)
    high, both = block[: 2 * half], block[2 * half :]
    first = jnp.round(both * (1 / 17.0))
    rest = jnp.concatenate([first, both - 17.0 * first])
    return high + high * rest * (1 / 2048.0)


def after(array, *others):
    return lax.optimization_barrier((array, *others))[0]


def tied(*arrays):
    return lax.optimization_barrier(arrays)


def gathered(queries, train_grads):
    rows, columns = queries.shape[0], train_grads.shape[0]
    half = rows // 2
    same, other = (jnp.zeros((8, rows, columns), jnp.float32) for _ in range(2))

    def add(part, slot, block):
        both = jnp.concatenate([block, swap(block, "c")])
        new = lax.dot_general(both, train_grads, (((1,), (1,)), ((), ())), preferred_element_type=jnp.float32)
        return lax.dynamic_update_slice(part, new.reshape(2, rows, columns), (slot, 0, 0))

    beside, near, back = swap(queries, "xl"), swap(queries, "y", 1), swap(queries, "y", 3)
    same = add(same, 0, queries)
    beside, near, back = tied(beside, near, back)
    near_beside, back_beside = swap(beside, "y", 1), swap(beside, "y", 3)
    same = add(same, 2, beside)
    same = add(same, 4, near)
    other = add(other, 4, back)
    near_beside, back_beside = tied(near_beside, back_beside)
    left = swap(jnp.concatenate([near[:half], near_beside[:half]]), "y", 3)
    right = swap(jnp.concatenate([back[half:], back_beside[half:]]), "y", 1)
    same = add(same, 6, near_beside)
    other = add(other, 6, back_beside)
    yield same
    (held,) = yield
    left, right = tied(left, right, held)[:2]
    other = add(other, 0, jnp.concatenate([left[:half], right[:half]]))
    other = add(other, 2, jnp.concatenate([left[half:], right[half:]]))
    yield other


class Ring:
    def __init__(self, part, long):
        self.ex = lax.axis_index("y") * 4 + lax.axis_index("xl") * 2 + lax.axis_index("c")
        self.z = lax.axis_index("z")
        self.part, self.long = part, long
        self.ahead = self.behind = None

    def term(self, distance):
        return lax.dynamic_index_in_dim(self.part, (self.z + distance) % 8 ^ self.ex % 8, 0, keepdims=False)

    def step(self, step):
        if step == 0:
            first = pack(self.term(4 * self.long))
            self.ahead = turn(first, self.long)
            return first
        hop = 4 - step
        ahead = unpack(self.ahead) + self.term(hop * self.long)
        behind = self.term(-hop * self.long)
        if step > 1:
            behind = unpack(self.behind) + behind
        if step == 3:
            return (ahead, behind) if self.long > 0 else (behind, ahead)
        ahead, behind = pack(ahead), pack(behind)
        return ahead, behind

    def send(self, ahead, behind):
        self.ahead, self.behind = turn(ahead, self.long), turn(behind, -self.long)


def on_device(queries, train_grads):
    flow = gathered(queries, train_grads)
    size = queries.shape[0] // PARTS

    def chains(i, part):
        return [Ring(part[:, k * size : k * size + size], 1 - 2 * (i ^ (k % 2))) for k in range(PARTS)]

    early = chains(0, next(flow))
    held = [ring.step(0) for ring in early]
    next(flow)
    late = chains(1, flow.send([held[0]]))
    firsts = [ring.step(0) for ring in late]
    if LATE:
        for ring, first in zip(early, firsts):
            ring.ahead = after(ring.ahead, firsts[0] if LATE == 1 else first)
    mine = lax.axis_index("xh") == lax.axis_index("y") // 2
    outs = [None] * PARTS
    for step in (1, 2):
        if step == 1:
            for k in range(PARTS):
                left, right = early[k].term(0), late[k].term(0)
                outs[k] = jnp.where(mine, left, right) + swap(jnp.where(mine, right, left), "xh")
        for k in range(PARTS):
            one, two = early[k].step(step), late[k].step(step)
            if SYNC:
                one, two = tied(one, two)
            else:
                one, two = tied(*one), tied(*two)
            early[k].send(*one)
            late[k].send(*two)
    for k in range(PARTS):
        one, two = early[k], late[k]
        one.ahead, outs[k] = tied(one.ahead, outs[k])
        sums = list(zip(one.step(3), two.step(3)))
        gives = tied(*(pack(jnp.where(mine, b, a)) for a, b in sums))
        keeps = [jnp.where(mine, a, b) + unpack(swap(give, "xh")) for (a, b), give in zip(sums, gives)]
        keeps = tied(*keeps)
        outs[k] += turn(keeps[0], 1) + turn(keeps[1], -1)
    return jnp.concatenate(outs)


def solution(mesh):
    fine = Mesh(mesh.devices.reshape(2, 8, 4, 2, 2), FEAT + EX)
    return jax.shard_map(
        on_device,
        mesh=fine,
        in_specs=(P(EX, FEAT), P(EX, FEAT)),
        out_specs=P(FEAT, EX),
        check_vma=False,
    )
```
